256 devices in a mesh: blk: 128 (over z, y, x_hi, core), dp: 2 (over x_lo).
Axes of the slice: x: 4 (x_hi: 2, x_lo: 2; x = x_hi * 2 + x_lo), y: 4, z: 8, core: 2. Of those that a mesh axis runs over, the one named last changes fastest.
Arguments:
- image_embed: bfloat16 [196608, 1152], P(('dp', 'blk')), parts along dimension 0, may hold values from -6 to 6
- text_embed: bfloat16 [196608, 1152], P(('dp', 'blk')), parts along dimension 0, may hold values from -6 to 6
- logit_scale: float32 [1], replicated, may hold values from 8 to 20
- logit_bias: float32 [1], replicated, may hold values from -1.5 to 0.5
Outputs:
- row_loss: float32 [196608], P(('dp', 'blk')), parts along dimension 0
- grad_image: float32 [196608, 1152], P(('dp', 'blk')), parts along dimension 0
- grad_text: float32 [196608, 1152], P(('dp', 'blk')), parts along dimension 0
The draws below stay inside these ranges and needn't reach their ends.
There are 2 independent parts, one for each index of `dp`. The reference program is written for one: setup_inputs(seed, part) draws one part's arguments, and reference() takes and returns one part's arrays. A program takes and returns all parts, laid end to end along the dimension named above; an argument that names none is the same for every part. Nothing has to cross between parts.
All inputs are finite; a program needn't handle non-finite values.
Results may differ from the reference program's by a relative error of at most 0.0046.
Values may be sent and summed in bfloat16 or wider, within the bound.
No kernel may reach another device: no remote copies, remote signals or barrier semaphores. Data moves between devices by JAX's collectives and lax.ppermute only.
A program may use at most 64 MiB of HBM per device.

```python
import math
import jax
import jax.numpy as jnp
from jax import lax

D = 1152
TOK_DEV = 768
TOKENS = 98304
N_BLK = 128


def shard_levels(rng, extent, split, smallest, high):
    def one(axis_at, blocks):
        draws = jax.random.uniform(jax.random.fold_in(jax.random.fold_in(rng, 6), axis_at), (blocks,), jnp.float32, smallest / len(split), high / len(split))
        return jnp.repeat(jnp.exp(draws), extent[axis_at] // blocks).reshape((-1,) + (1,) * (len(extent) - axis_at - 1))

    gain = one(*split[0])
    for cut in split[1:]:
        gain = gain * one(*cut)
    return gain


def scatter_about(own_key, dims, spread, limit, shards=(), held_as=jnp.bfloat16):
    values = spread * jax.random.normal(own_key, dims, jnp.float32)
    if shards:
        values = values * shard_levels(own_key, dims, shards, -0.22, 0.18)
    return jnp.clip(values, -limit, limit).astype(held_as)


def setup_inputs(seed: int = 0, part: int = 0) -> dict:
    splits = jax.random.split(jax.random.key(seed), 5)
    part_keys = jax.random.split(jax.random.fold_in(splits[4], part), 5)
    image_embed = scatter_about(part_keys[0], (TOKENS, D), 1.0, 6.0, ((0, 128),))
    text_embed = scatter_about(part_keys[1], (TOKENS, D), 1.0, 6.0, ((0, 128),))
    logit_scale = jnp.clip(jnp.exp(jax.random.uniform(splits[2], (1,), jnp.float32, math.log(8.0), math.log(20.0))), 8.0, 20.0)
    logit_bias = jnp.clip(jax.random.uniform(splits[3], (1,), jnp.float32, -1.5, 0.5), -1.5, 0.5)
    return dict(image_embed=image_embed, text_embed=text_embed, logit_scale=logit_scale, logit_bias=logit_bias)


EPS = 1e-06

def normalize(x):
    xf = x.astype(jnp.float32)
    inv = lax.rsqrt(lax.optimization_barrier(jnp.sum(xf * xf, axis=-1, keepdims=True)) + EPS)
    return (xf * inv, inv)

def tile_terms(left, right, scale, bias, sign):
    logits = scale * jnp.dot(left, right.T, preferred_element_type=jnp.float32) + bias
    losses = lax.optimization_barrier(jnp.sum(jax.nn.softplus(-sign * logits), axis=1))
    coef = (-scale * sign * jax.nn.sigmoid(-sign * logits)).astype(jnp.bfloat16)
    return (losses, coef)

def unnormalize(unit, inv, grad):
    return inv * (grad - unit * lax.optimization_barrier(jnp.sum(unit * grad, axis=-1, keepdims=True)))

def reference(image_embed, text_embed, logit_scale, logit_bias):
    scale = logit_scale[0]
    bias = logit_bias[0]
    img_unit, inv_img = normalize(image_embed)
    txt_unit, inv_txt = normalize(text_embed)
    img_low = img_unit.astype(jnp.bfloat16)
    txt_low = txt_unit.astype(jnp.bfloat16)
    blocks = N_BLK
    img_blocks = img_low.reshape(blocks, TOK_DEV, D)
    txt_blocks = txt_low.reshape(blocks, TOK_DEV, D)
    rows = jnp.arange(TOK_DEV, dtype=jnp.int32)
    diag_sign = jnp.where(rows[:, None] == rows[None, :], 1.0, -1.0).astype(jnp.float32)

    def per_block(index):
        left = img_blocks[index]
        total_loss = jnp.zeros((TOK_DEV,), jnp.float32)
        g_img = jnp.zeros((TOK_DEV, D), jnp.float32)
        text_terms = []
        for step in range(3):
            right = txt_blocks[(index - step) % blocks]
            sign = diag_sign if step == 0 else jnp.float32(-1.0)
            losses, coef = tile_terms(left, right, scale, bias, sign)
            total_loss = total_loss + losses
            g_img = g_img + jnp.dot(coef, right, preferred_element_type=jnp.float32)
            text_terms.append(jnp.dot(coef.T, left, preferred_element_type=jnp.float32))
        return (total_loss, g_img, text_terms[0], text_terms[1], text_terms[2])
    losses, g_img, term_own, term_one, term_two = lax.map(per_block, jnp.arange(blocks, dtype=jnp.int32))
    g_txt = term_own + jnp.roll(term_one, -1, axis=0) + jnp.roll(term_two, -2, axis=0)
    row_loss = losses.reshape(TOKENS) / (3 * TOK_DEV)
    grad_image = unnormalize(img_unit, inv_img, g_img.reshape(TOKENS, D))
    grad_text = unnormalize(txt_unit, inv_txt, g_txt.reshape(TOKENS, D))
    return (row_loss, grad_image, grad_text)
```

```python
import jax
import jax.numpy as jnp
from jax import lax
from jax.sharding import PartitionSpec as P

EPS = 1e-06
CHUNKS = 4


def normalize(x):
    xf = x.astype(jnp.float32)
    inv = lax.rsqrt(jnp.sum(xf * xf, axis=-1, keepdims=True) + EPS)
    return (xf * inv, inv)


def unnormalize(unit, inv, grad):
    return inv * (grad - unit * jnp.sum(unit * grad, axis=-1, keepdims=True))


def dot_rows(a, b):
    return lax.dot_general(a, b, (((1,), (1,)), ((), ())), preferred_element_type=jnp.float32)


def own_tile(mine, other, scale, bias):
    rows = lax.iota(jnp.int32, mine.shape[0])
    sign = jnp.where(rows[:, None] == rows[None, :], 1.0, -1.0).astype(jnp.float32)
    logits = scale * dot_rows(mine, other) + bias
    loss = jax.nn.softplus(-sign * logits)
    coef = (-scale * sign * jax.nn.sigmoid(-sign * logits)).astype(jnp.bfloat16)
    grad_mine = jnp.dot(coef, other, preferred_element_type=jnp.float32)
    grad_other = lax.dot_general(coef, mine, (((0,), (0,)), ((), ())), preferred_element_type=jnp.float32)
    return grad_mine, grad_other, jnp.sum(loss, axis=1), jnp.sum(loss, axis=0)


def foreign_tile(mine, raw, scale, bias):
    other = normalize(raw)[0].astype(jnp.bfloat16)
    logits = scale * dot_rows(mine, other) + bias
    coef = (scale * jax.nn.sigmoid(logits)).astype(jnp.bfloat16)
    return jnp.dot(coef, other, preferred_element_type=jnp.float32), jnp.sum(jax.nn.softplus(logits), axis=1)


def shards(image_embed, text_embed, logit_scale, logit_bias):
    scale = logit_scale[0]
    bias = logit_bias[0]
    rows = image_embed.shape[0]
    count = lax.axis_size("blk")
    facing = [(b, (b + 1) % count if b % 2 else (b - 1) % count) for b in range(count)]
    inside = [(b, b + 1 - 2 * (b % 2)) for b in range(count)]
    far = [(b, (b - 2) % count if b % 2 else (b + 2) % count) for b in range(count)]
    odd = lax.axis_index("blk") % 2 == 1

    first = jnp.where(odd, text_embed, image_embed)
    second = jnp.where(odd, image_embed, text_embed)
    one = lax.ppermute(first, "blk", facing)
    zero = lax.ppermute(second, "blk", inside)
    two = lax.ppermute(one, "blk", inside)
    held, one = lax.optimization_barrier((second, one))
    step = rows // CHUNKS
    three = [lax.ppermute(held[i * step : (i + 1) * step], "blk", far) for i in range(CHUNKS)]

    first_unit, first_inv = normalize(first)
    second_unit, second_inv = normalize(second)
    first_low = first_unit.astype(jnp.bfloat16)
    second_low = second_unit.astype(jnp.bfloat16)
    first_grad, second_grad, first_loss, second_loss = own_tile(first_low, second_low, scale, bias)
    for raw in (zero, two):
        grad, loss = foreign_tile(second_low, raw, scale, bias)
        second_grad, second_loss = second_grad + grad, second_loss + loss
    for raw in [one] + three:
        grad, loss = foreign_tile(first_low, raw, scale, bias)
        first_grad, first_loss = first_grad + grad, first_loss + loss
    first_out = unnormalize(first_unit, first_inv, first_grad)
    second_out = unnormalize(second_unit, second_inv, second_grad)
    row_loss = jnp.where(odd, second_loss, first_loss) / (3 * rows)
    return (row_loss, jnp.where(odd, second_out, first_out), jnp.where(odd, first_out, second_out))


def solution(mesh):
    in_specs = (P(("dp", "blk"), None), P(("dp", "blk"), None), P(), P())
    out_specs = (P(("dp", "blk")), P(("dp", "blk"), None), P(("dp", "blk"), None))
    return jax.shard_map(shards, mesh=mesh, in_specs=in_specs, out_specs=out_specs, check_vma=False)
```

```python
import functools

import jax
import jax.numpy as jnp
from jax import lax
from jax.experimental import pallas as pl
from jax.experimental.pallas import tpu as pltpu
from jax.sharding import PartitionSpec as P

EPS = 1e-06
CUTS = (512, 256)
BLOCK = 256
LANES = 128
PART = 256


def inverse_norm(x):
    return lax.rsqrt(jnp.sum(x * x, axis=-1, keepdims=True) + EPS)


def dot_rows(a, b):
    return lax.dot_general(a, b, (((1,), (1,)), ((), ())), preferred_element_type=jnp.float32)


def blocks(ref):
    return [pl.ds(start, BLOCK) for start in range(0, ref.shape[0], BLOCK)]


def normalize_parts(parts, low):
    start = 0
    for part in parts:
        normalize_into(part, low.at[pl.ds(start, part.shape[0])])
        start += part.shape[0]


def normalize_into(raw, low, inv=None):
    for at in blocks(raw):
        x = raw[at, :].astype(jnp.float32)
        scaled = inverse_norm(x)
        low[at, :] = (x * scaled).astype(jnp.bfloat16)
        if inv is not None:
            inv[at, :] = scaled


def pair_terms(logits, scale, diagonal=None):
    if diagonal is not None:
        logits = jnp.where(diagonal, -logits, logits)
        scale = jnp.where(diagonal, -scale, scale)
    up = jnp.exp(logits)
    coef = (scale * (up / (1.0 + up))).astype(jnp.bfloat16)
    return coef, jnp.sum(jnp.log1p(up), axis=1, keepdims=True)


def own_kernel(scalars, first, second, first_low, second_low, first_inv, second_inv, first_grad, second_grad, first_loss, second_loss):
    scale, bias = scalars[0], scalars[1]
    normalize_into(first, first_low, first_inv)
    normalize_into(second, second_low, second_inv)
    for low, other, grad, loss in (
        (first_low, second_low, first_grad, first_loss),
        (second_low, first_low, second_grad, second_loss),
    ):
        for at in blocks(low):
            logits = scale * dot_rows(low[at, :], other[...]) + bias
            row = at.start + lax.broadcasted_iota(jnp.int32, logits.shape, 0)
            diagonal = row == lax.broadcasted_iota(jnp.int32, logits.shape, 1)
            coef, loss[at, :] = pair_terms(logits, scale, diagonal)
            grad[at, :] = jnp.dot(coef, other[...], preferred_element_type=jnp.float32)


def tile_block(at, scalars, low, other, grad, loss):
    scale, bias = scalars[0], scalars[1]
    coef, losses = pair_terms(scale * dot_rows(low[at, :], other[...]) + bias, scale)
    return grad[at, :] + jnp.dot(coef, other[...], preferred_element_type=jnp.float32), loss[at, :] + losses


def add_kernel(scalars, low, grad, loss, *rest):
    *parts, grad_out, loss_out, other = rest
    normalize_parts(parts, other)
    add_low_kernel(scalars, low, grad, loss, other, grad_out, loss_out)


def add_low_kernel(scalars, low, grad, loss, other, grad_out, loss_out):
    for at in blocks(low):
        grad_out[at, :], loss_out[at, :] = tile_block(at, scalars, low, other, grad, loss)


def finish_rows(at, step, place, total, raw, inv, even_out, odd_out, held, sems):
    unit = raw[at, :].astype(jnp.float32) * inv[at, :]
    held[at, :] = inv[at, :] * (total - unit * jnp.sum(unit * total, axis=-1, keepdims=True))
    pair = [pltpu.make_async_copy(held.at[at], out.at[at], sems.at[step]) for out in (even_out, odd_out)]
    pl.when(place[0] == 0)(pair[0].start)
    pl.when(place[0] != 0)(pair[1].start)
    return pair


def wait_for(place, copies):
    for pair in copies:
        pl.when(place[0] == 0)(pair[0].wait)
        pl.when(place[0] != 0)(pair[1].wait)


def second_kernel(scalars, place, low, grad, loss, raw, inv, *rest):
    *parts, even_out, odd_out, loss_out, held, sems, other = rest
    normalize_parts(parts, other)
    copies = []
    for step, at in enumerate(blocks(low)):
        total, loss_out[at, :] = tile_block(at, scalars, low, other, grad, loss)
        copies.append(finish_rows(at, step, place, total, raw, inv, even_out, odd_out, held, sems))
    wait_for(place, copies)


def first_kernel(scalars, place, low, other, grad, loss, raw, inv, second_loss, even_in, odd_in, even_out, odd_out, loss_out, held, sems):
    copies = []
    for step, at in enumerate(blocks(low)):
        total, losses = tile_block(at, scalars, low, other, grad, loss)
        copies.append(finish_rows(at, step, place, total, raw, inv, even_out, odd_out, held, sems))
        losses = jnp.where(place[0] == 0, losses, second_loss[at, :]) / (3 * low.shape[0])
        loss_out[at] = jnp.transpose(jnp.broadcast_to(losses, (BLOCK, LANES)))[0]
    wait_for(place, copies)


VMEM = pl.BlockSpec(memory_space=pltpu.VMEM)
SMEM = pl.BlockSpec(memory_space=pltpu.SMEM)
ANY = pl.BlockSpec(memory_space=pl.ANY)
PARAMS = pltpu.CompilerParams(vmem_limit_bytes=24 * 1024 * 1024)


COST = pl.CostEstimate(flops=1, bytes_accessed=1, transcendentals=0)


def like(*arrays):
    return tuple(jax.ShapeDtypeStruct(a.shape, a.dtype) for a in arrays)


def own_tile(scalars, first, second):
    grad = jax.ShapeDtypeStruct(first.shape, jnp.float32)
    column = jax.ShapeDtypeStruct((first.shape[0], 1), jnp.float32)
    return pl.pallas_call(
        own_kernel,
        out_shape=(*like(first, second), column, column, grad, grad, column, column),
        in_specs=[SMEM, VMEM, VMEM],
        out_specs=(VMEM,) * 8,
        cost_estimate=COST,
        compiler_params=PARAMS,
        name="own_tile",
    )(scalars, first, second)


def add_tile(scalars, low, grad, loss, parts, raw):
    return pl.pallas_call(
        add_kernel if raw else add_low_kernel,
        out_shape=like(grad, loss),
        in_specs=[SMEM, VMEM, VMEM, VMEM] + [VMEM] * len(parts),
        out_specs=(VMEM, VMEM),
        scratch_shapes=[pltpu.VMEM(low.shape, low.dtype)] if raw else [],
        input_output_aliases={2: 0, 3: 1},
        cost_estimate=COST,
        compiler_params=PARAMS,
        name="add_tile",
    )(scalars, low, grad, loss, *parts)


def second_tile(scalars, place, low, grad, loss, raw, inv, parts):
    return pl.pallas_call(
        second_kernel,
        out_shape=like(grad, grad, loss),
        in_specs=[SMEM, SMEM] + [VMEM] * (5 + len(parts)),
        out_specs=(ANY, ANY, VMEM),
        scratch_shapes=[
            pltpu.VMEM(grad.shape, grad.dtype),
            pltpu.SemaphoreType.DMA((low.shape[0] // BLOCK,)),
            pltpu.VMEM(low.shape, low.dtype),
        ],
        cost_estimate=COST,
        compiler_params=PARAMS,
        name="second_tile",
    )(scalars, place, low, grad, loss, raw, inv, *parts)


def first_tile(scalars, place, low, other, grad, loss, raw, inv, second_loss, outs):
    return pl.pallas_call(
        first_kernel,
        out_shape=(*like(grad, grad), jax.ShapeDtypeStruct(low.shape[:1], jnp.float32)),
        in_specs=[SMEM, SMEM] + [VMEM] * 7 + [ANY, ANY],
        out_specs=(ANY, ANY, VMEM),
        scratch_shapes=[pltpu.VMEM(grad.shape, grad.dtype), pltpu.SemaphoreType.DMA((low.shape[0] // BLOCK,))],
        input_output_aliases={9: 0, 10: 1},
        cost_estimate=COST,
        compiler_params=PARAMS,
        name="first_tile",
    )(scalars, place, low, other, grad, loss, raw, inv, second_loss, *outs)


def shards(image_embed, text_embed, logit_scale, logit_bias):
    scalars = jnp.concatenate([logit_scale, logit_bias])
    count = lax.axis_size("blk")
    facing = [(b, (b + 1) % count if b % 2 else (b - 1) % count) for b in range(count)]
    inside = [(b, b + 1 - 2 * (b % 2)) for b in range(count)]
    far = [(b, (b - 2) % count if b % 2 else (b + 2) % count) for b in range(count)]
    hold = lax.optimization_barrier
    parity = (lax.axis_index("blk") % 2).astype(jnp.int32)
    odd = parity == 1

    def across(value):
        return [lax.ppermute(value[start : start + PART], "blk", inside) for start in range(0, value.shape[0], PART)]

    first = hold(jnp.where(odd, text_embed, image_embed))
    one = lax.ppermute(first, "blk", facing)
    image_embed, text_embed, first = hold((image_embed, text_embed, first))
    second = hold(jnp.where(odd, image_embed, text_embed))
    zero = across(second)
    first_low, second_low, first_inv, second_inv, first_grad, second_grad, first_loss, second_loss = own_tile(scalars, first, second)
    second_grad, second_loss = add_tile(scalars, second_low, second_grad, second_loss, zero, True)

    piece, second_loss = hold((second_low[: CUTS[0]], second_loss))
    three = lax.ppermute(piece, "blk", far)
    one, second_loss = hold((one, second_loss))
    two = across(one)
    piece, one = hold((second_low[CUTS[0] :], one))
    four = lax.ppermute(piece, "blk", far)
    first_grad, first_loss = add_tile(scalars, first_low, first_grad, first_loss, [one], True)
    *two, first_loss = hold((*two, first_loss))
    *outs, second_loss = second_tile(scalars, 1 - parity[None], second_low, second_grad, second_loss, second, second_inv, two)
    three, second_loss = hold((three, second_loss))
    first_grad, first_loss = add_tile(scalars, first_low, first_grad, first_loss, [three], False)
    grad_image, grad_text, row_loss = first_tile(
        scalars, parity[None], first_low, four, first_grad, first_loss, first, first_inv, second_loss, outs
    )
    return (row_loss, grad_image, grad_text)


def solution(mesh):
    in_specs = (P(("dp", "blk"), None), P(("dp", "blk"), None), P(), P())
    out_specs = (P(("dp", "blk")), P(("dp", "blk"), None), P(("dp", "blk"), None))
    return jax.shard_map(shards, mesh=mesh, in_specs=in_specs, out_specs=out_specs, check_vma=False)
```

```python
import functools

import jax
import jax.numpy as jnp
from jax import lax
from jax.experimental import pallas as pl
from jax.experimental.pallas import tpu as pltpu
from jax.sharding import PartitionSpec as P

EPS = 1e-06
HEADS = (256, 512)
CUTS = (384, 384)
BLOCK = 384
LANES = 128
PART = 256


def inverse_norm(x):
    return lax.rsqrt(jnp.sum(x * x, axis=-1, keepdims=True) + EPS)


def dot_rows(a, b):
    return lax.dot_general(a, b, (((1,), (1,)), ((), ())), preferred_element_type=jnp.float32)


def blocks(ref):
    step = ref.shape[0] // pl.cdiv(ref.shape[0], BLOCK)
    return [pl.ds(start, step) for start in range(0, ref.shape[0], step)]


def normalize_parts(parts, low):
    start = 0
    for part in parts:
        normalize_into(part, low.at[pl.ds(start, part.shape[0])])
        start += part.shape[0]


def normalize_into(raw, low, inv=None):
    for at in blocks(raw):
        x = raw[at, :].astype(jnp.float32)
        scaled = inverse_norm(x)
        low[at, :] = (x * scaled).astype(jnp.bfloat16)
        if inv is not None:
            inv[at, :] = scaled


def pair_terms(logits, scale, diagonal=None):
    if diagonal is not None:
        logits = jnp.where(diagonal, -logits, logits)
        scale = jnp.where(diagonal, -scale, scale)
    up = jnp.exp(logits)
    coef = (scale * (up / (1.0 + up))).astype(jnp.bfloat16)
    return coef, jnp.sum(jnp.log1p(up), axis=1, keepdims=True)


def own_kernel(scalars, first_a, first_b, second, first, first_low, second_low, first_inv, second_inv, first_grad, second_grad, first_loss, second_loss):
    scale, bias = scalars[0], scalars[1]
    split = first_a.shape[0]
    first[:split, :] = first_a[...]
    first[split:, :] = first_b[...]
    normalize_into(first, first_low, first_inv)
    normalize_into(second, second_low, second_inv)
    for low, other, grad, loss in (
        (first_low, second_low, first_grad, first_loss),
        (second_low, first_low, second_grad, second_loss),
    ):
        for at in blocks(low):
            logits = scale * dot_rows(low[at, :], other[...]) + bias
            row = at.start + lax.broadcasted_iota(jnp.int32, logits.shape, 0)
            diagonal = row == lax.broadcasted_iota(jnp.int32, logits.shape, 1)
            coef, loss[at, :] = pair_terms(logits, scale, diagonal)
            grad[at, :] = jnp.dot(coef, other[...], preferred_element_type=jnp.float32)


def coefficients(scalars, low, other):
    scale, bias = scalars[0], scalars[1]
    return [(at, *pair_terms(scale * dot_rows(low[at, :], other[...]) + bias, scale)) for at in blocks(low)]


def add_kernel(scalars, low, grad, loss, *rest):
    *parts, grad_out, loss_out, other = rest
    normalize_parts(parts, other)
    add_low_kernel(scalars, low, grad, loss, other, grad_out, loss_out)


def add_low_kernel(scalars, low, grad, loss, other, grad_out, loss_out):
    for at, coef, losses in coefficients(scalars, low, other):
        grad_out[at, :] = grad[at, :] + jnp.dot(coef, other[...], preferred_element_type=jnp.float32)
        loss_out[at, :] = loss[at, :] + losses


def finish(place, terms, other, grad, raw, inv, even_out, odd_out, held, sems):
    copies = []
    for step, (at, coef, _) in enumerate(terms):
        total = grad[at, :] + jnp.dot(coef, other[...], preferred_element_type=jnp.float32)
        unit = raw[at, :].astype(jnp.float32) * inv[at, :]
        held[at, :] = inv[at, :] * (total - unit * jnp.sum(unit * total, axis=-1, keepdims=True))
        copies.append([pltpu.make_async_copy(held.at[at], out.at[at], sems.at[step]) for out in (even_out, odd_out)])
        pl.when(place[0] == 0)(copies[-1][0].start)
        pl.when(place[0] != 0)(copies[-1][1].start)
    return copies


def wait_for(place, copies):
    for pair in copies:
        pl.when(place[0] == 0)(pair[0].wait)
        pl.when(place[0] != 0)(pair[1].wait)


def second_kernel(scalars, place, low, grad, loss, raw, inv, *rest):
    *parts, even_out, odd_out, loss_out, held, sems, other = rest
    normalize_parts(parts, other)
    terms = coefficients(scalars, low, other)
    copies = finish(place, terms, other, grad, raw, inv, even_out, odd_out, held, sems)
    for at, _, losses in terms:
        loss_out[at, :] = loss[at, :] + losses
    wait_for(place, copies)


def first_kernel(scalars, place, low, other, grad, loss, raw, inv, second_loss, even_in, odd_in, even_out, odd_out, loss_out, held, sems):
    terms = coefficients(scalars, low, other)
    copies = finish(place, terms, other, grad, raw, inv, even_out, odd_out, held, sems)
    for at, _, losses in terms:
        chosen = jnp.where(place[0] == 0, loss[at, :] + losses, second_loss[at, :]) / (3 * low.shape[0])
        loss_out[at] = jnp.transpose(jnp.broadcast_to(chosen, (BLOCK, LANES)))[0]
    wait_for(place, copies)


VMEM = pl.BlockSpec(memory_space=pltpu.VMEM)
SMEM = pl.BlockSpec(memory_space=pltpu.SMEM)
ANY = pl.BlockSpec(memory_space=pl.ANY)
PARAMS = pltpu.CompilerParams(vmem_limit_bytes=24 * 1024 * 1024)


COST = pl.CostEstimate(flops=1, bytes_accessed=1, transcendentals=0)


def like(*arrays):
    return tuple(jax.ShapeDtypeStruct(a.shape, a.dtype) for a in arrays)


def own_tile(scalars, first_a, first_b, second):
    grad = jax.ShapeDtypeStruct(second.shape, jnp.float32)
    column = jax.ShapeDtypeStruct((second.shape[0], 1), jnp.float32)
    return pl.pallas_call(
        own_kernel,
        out_shape=(*like(second, second, second), column, column, grad, grad, column, column),
        in_specs=[SMEM, VMEM, VMEM, VMEM],
        out_specs=(VMEM,) * 9,
        cost_estimate=COST,
        compiler_params=PARAMS,
        name="own_tile",
    )(scalars, first_a, first_b, second)


def add_tile(scalars, low, grad, loss, parts, raw):
    return pl.pallas_call(
        add_kernel if raw else add_low_kernel,
        out_shape=like(grad, loss),
        in_specs=[SMEM] + [VMEM] * (3 + len(parts)),
        out_specs=(VMEM, VMEM),
        scratch_shapes=[pltpu.VMEM((sum(p.shape[0] for p in parts), low.shape[1]), low.dtype)] if raw else [],
        input_output_aliases={2: 0, 3: 1},
        cost_estimate=COST,
        compiler_params=PARAMS,
        name="add_tile",
    )(scalars, low, grad, loss, *parts)


def second_tile(scalars, place, low, grad, loss, raw, inv, parts):
    return pl.pallas_call(
        second_kernel,
        out_shape=like(grad, grad, loss),
        in_specs=[SMEM, SMEM] + [VMEM] * (5 + len(parts)),
        out_specs=(ANY, ANY, VMEM),
        scratch_shapes=[
            pltpu.VMEM(grad.shape, grad.dtype),
            pltpu.SemaphoreType.DMA((low.shape[0] // BLOCK,)),
            pltpu.VMEM((sum(p.shape[0] for p in parts), low.shape[1]), low.dtype),
        ],
        cost_estimate=COST,
        compiler_params=PARAMS,
        name="second_tile",
    )(scalars, place, low, grad, loss, raw, inv, *parts)


def first_tile(scalars, place, low, other, grad, loss, raw, inv, second_loss, outs):
    return pl.pallas_call(
        first_kernel,
        out_shape=(*like(grad, grad), jax.ShapeDtypeStruct(low.shape[:1], jnp.float32)),
        in_specs=[SMEM, SMEM] + [VMEM] * 7 + [ANY, ANY],
        out_specs=(ANY, ANY, VMEM),
        scratch_shapes=[pltpu.VMEM(grad.shape, grad.dtype), pltpu.SemaphoreType.DMA((low.shape[0] // BLOCK,))],
        input_output_aliases={9: 0, 10: 1},
        cost_estimate=COST,
        compiler_params=PARAMS,
        name="first_tile",
    )(scalars, place, low, other, grad, loss, raw, inv, second_loss, *outs)


def shards(image_embed, text_embed, logit_scale, logit_bias):
    scalars = jnp.concatenate([logit_scale, logit_bias])
    count = lax.axis_size("blk")
    facing = [(b, (b + 1) % count if b % 2 else (b - 1) % count) for b in range(count)]
    inside = [(b, b + 1 - 2 * (b % 2)) for b in range(count)]
    far = [(b, (b - 2) % count if b % 2 else (b + 2) % count) for b in range(count)]
    hold = lax.optimization_barrier
    parity = (lax.axis_index("blk") % 2).astype(jnp.int32)
    odd = parity == 1

    def across(value):
        return [lax.ppermute(value[start : start + PART], "blk", inside) for start in range(0, value.shape[0], PART)]

    split = HEADS[0]
    first_a = hold(jnp.where(odd, text_embed[:split], image_embed[:split]))
    one_a = lax.ppermute(first_a, "blk", facing)
    image_embed, text_embed, first_a = hold((image_embed, text_embed, first_a))
    first_b = hold(jnp.where(odd, text_embed[split:], image_embed[split:]))
    one_b = lax.ppermute(first_b, "blk", facing)
    image_embed, text_embed, first_b = hold((image_embed, text_embed, first_b))
    second = hold(jnp.where(odd, image_embed, text_embed))
    zero = across(second)
    first, first_low, second_low, first_inv, second_inv, first_grad, second_grad, first_loss, second_loss = own_tile(
        scalars, first_a, first_b, second
    )
    second_grad, second_loss = add_tile(scalars, second_low, second_grad, second_loss, zero, True)
    piece, second_loss = hold((second_low[: CUTS[0]], second_loss))
    late_a = lax.ppermute(piece, "blk", far)

    one_a, second_loss = hold((one_a, second_loss))
    two_a = across(one_a)
    first_grad, first_loss = add_tile(scalars, first_low, first_grad, first_loss, [one_a], True)
    *two_a, first_loss = hold((*two_a, first_loss))
    second_grad, second_loss = add_tile(scalars, second_low, second_grad, second_loss, two_a, True)

    one_b, second_loss = hold((one_b, second_loss))
    two_b = across(one_b)
    piece, one_b = hold((second_low[-CUTS[1] :], one_b))
    late_b = lax.ppermute(piece, "blk", far)
    first_grad, first_loss = add_tile(scalars, first_low, first_grad, first_loss, [one_b], True)
    *two_b, first_loss = hold((*two_b, first_loss))
    *outs, second_loss = second_tile(scalars, 1 - parity[None], second_low, second_grad, second_loss, second, second_inv, two_b)
    late_a, second_loss = hold((late_a, second_loss))
    first_grad, first_loss = add_tile(scalars, first_low, first_grad, first_loss, [late_a], False)

    grad_image, grad_text, row_loss = first_tile(
        scalars, parity[None], first_low, late_b, first_grad, first_loss, first, first_inv, second_loss, outs
    )
    return (row_loss, grad_image, grad_text)


def solution(mesh):
    in_specs = (P(("dp", "blk"), None), P(("dp", "blk"), None), P(), P())
    out_specs = (P(("dp", "blk")), P(("dp", "blk"), None), P(("dp", "blk"), None))
    return jax.shard_map(shards, mesh=mesh, in_specs=in_specs, out_specs=out_specs, check_vma=False)
```

```python
import functools

import jax
import jax.numpy as jnp
from jax import lax
from jax.experimental import pallas as pl
from jax.experimental.pallas import tpu as pltpu
from jax.sharding import PartitionSpec as P

EPS = 1e-06
HEADS = (384, 384)
CUTS = (512, 256)
BLOCK = 384
LANES = 128
PART = 256
TAIL_PART = 192


def inverse_norm(x):
    return lax.rsqrt(jnp.sum(x * x, axis=-1, keepdims=True) + EPS)


def dot_rows(a, b):
    return lax.dot_general(a, b, (((1,), (1,)), ((), ())), preferred_element_type=jnp.float32)


def blocks(ref):
    step = ref.shape[0] // pl.cdiv(ref.shape[0], BLOCK)
    return [pl.ds(start, step) for start in range(0, ref.shape[0], step)]


def normalize_parts(parts, low):
    start = 0
    for part in parts:
        normalize_into(part, low.at[pl.ds(start, part.shape[0])])
        start += part.shape[0]


def normalize_into(raw, low, inv=None):
    for at in blocks(raw):
        x = raw[at, :].astype(jnp.float32)
        scaled = inverse_norm(x)
        low[at, :] = (x * scaled).astype(jnp.bfloat16)
        if inv is not None:
            inv[at, :] = scaled


def pair_terms(logits, scale, diagonal=None):
    if diagonal is not None:
        logits = jnp.where(diagonal, -logits, logits)
        scale = jnp.where(diagonal, -scale, scale)
    up = jnp.exp(logits)
    coef = (scale * (up / (1.0 + up))).astype(jnp.bfloat16)
    return coef, jnp.sum(jnp.log1p(up), axis=1, keepdims=True)


def own_kernel(scalars, first_a, first_b, second, first, first_low, second_low, first_inv, second_inv, first_grad, second_grad, first_loss, second_loss):
    scale, bias = scalars[0], scalars[1]
    split = first_a.shape[0]
    first[:split, :] = first_a[...]
    first[split:, :] = first_b[...]
    normalize_into(first, first_low, first_inv)
    normalize_into(second, second_low, second_inv)
    for low, other, grad, loss in (
        (first_low, second_low, first_grad, first_loss),
        (second_low, first_low, second_grad, second_loss),
    ):
        for at in blocks(low):
            logits = scale * dot_rows(low[at, :], other[...]) + bias
            row = at.start + lax.broadcasted_iota(jnp.int32, logits.shape, 0)
            diagonal = row == lax.broadcasted_iota(jnp.int32, logits.shape, 1)
            coef, loss[at, :] = pair_terms(logits, scale, diagonal)
            grad[at, :] = jnp.dot(coef, other[...], preferred_element_type=jnp.float32)


def coefficients(scalars, low, other):
    scale, bias = scalars[0], scalars[1]
    return [(at, *pair_terms(scale * dot_rows(low[at, :], other[...]) + bias, scale)) for at in blocks(low)]


def add_kernel(scalars, low, grad, loss, *rest):
    *parts, grad_out, loss_out, other = rest
    normalize_parts(parts, other)
    add_low_kernel(scalars, low, grad, loss, other, grad_out, loss_out)


def add_low_kernel(scalars, low, grad, loss, other, grad_out, loss_out):
    for at, coef, losses in coefficients(scalars, low, other):
        grad_out[at, :] = grad[at, :] + jnp.dot(coef, other[...], preferred_element_type=jnp.float32)
        loss_out[at, :] = loss[at, :] + losses


def finish(place, terms, other, grad, raw, inv, even_out, odd_out, held, sems):
    copies = []
    for step, (at, coef, _) in enumerate(terms):
        total = grad[at, :] + jnp.dot(coef, other[...], preferred_element_type=jnp.float32)
        unit = raw[at, :].astype(jnp.float32) * inv[at, :]
        held[at, :] = inv[at, :] * (total - unit * jnp.sum(unit * total, axis=-1, keepdims=True))
        copies.append([pltpu.make_async_copy(held.at[at], out.at[at], sems.at[step]) for out in (even_out, odd_out)])
        pl.when(place[0] == 0)(copies[-1][0].start)
        pl.when(place[0] != 0)(copies[-1][1].start)
    return copies


def wait_for(place, copies):
    for pair in copies:
        pl.when(place[0] == 0)(pair[0].wait)
        pl.when(place[0] != 0)(pair[1].wait)


def second_kernel(scalars, place, low, grad, loss, raw, inv, *rest):
    *parts, even_out, odd_out, loss_out, held, sems, other = rest
    normalize_parts(parts, other)
    terms = coefficients(scalars, low, other)
    copies = finish(place, terms, other, grad, raw, inv, even_out, odd_out, held, sems)
    for at, _, losses in terms:
        loss_out[at, :] = loss[at, :] + losses
    wait_for(place, copies)


def first_kernel(scalars, place, low, other, grad, loss, raw, inv, second_loss, even_in, odd_in, even_out, odd_out, loss_out, held, sems):
    terms = coefficients(scalars, low, other)
    copies = finish(place, terms, other, grad, raw, inv, even_out, odd_out, held, sems)
    for at, _, losses in terms:
        chosen = jnp.where(place[0] == 0, loss[at, :] + losses, second_loss[at, :]) / (3 * low.shape[0])
        loss_out[at] = jnp.transpose(jnp.broadcast_to(chosen, (BLOCK, LANES)))[0]
    wait_for(place, copies)


VMEM = pl.BlockSpec(memory_space=pltpu.VMEM)
SMEM = pl.BlockSpec(memory_space=pltpu.SMEM)
ANY = pl.BlockSpec(memory_space=pl.ANY)
PARAMS = pltpu.CompilerParams(vmem_limit_bytes=24 * 1024 * 1024)


COST = pl.CostEstimate(flops=1, bytes_accessed=1, transcendentals=0)


def like(*arrays):
    return tuple(jax.ShapeDtypeStruct(a.shape, a.dtype) for a in arrays)


def own_tile(scalars, first_a, first_b, second):
    grad = jax.ShapeDtypeStruct(second.shape, jnp.float32)
    column = jax.ShapeDtypeStruct((second.shape[0], 1), jnp.float32)
    return pl.pallas_call(
        own_kernel,
        out_shape=(*like(second, second, second), column, column, grad, grad, column, column),
        in_specs=[SMEM, VMEM, VMEM, VMEM],
        out_specs=(VMEM,) * 9,
        cost_estimate=COST,
        compiler_params=PARAMS,
        name="own_tile",
    )(scalars, first_a, first_b, second)


def add_tile(scalars, low, grad, loss, parts, raw):
    return pl.pallas_call(
        add_kernel if raw else add_low_kernel,
        out_shape=like(grad, loss),
        in_specs=[SMEM] + [VMEM] * (3 + len(parts)),
        out_specs=(VMEM, VMEM),
        scratch_shapes=[pltpu.VMEM((sum(p.shape[0] for p in parts), low.shape[1]), low.dtype)] if raw else [],
        input_output_aliases={2: 0, 3: 1},
        cost_estimate=COST,
        compiler_params=PARAMS,
        name="add_tile",
    )(scalars, low, grad, loss, *parts)


def second_tile(scalars, place, low, grad, loss, raw, inv, parts):
    return pl.pallas_call(
        second_kernel,
        out_shape=like(grad, grad, loss),
        in_specs=[SMEM, SMEM] + [VMEM] * (5 + len(parts)),
        out_specs=(ANY, ANY, VMEM),
        scratch_shapes=[
            pltpu.VMEM(grad.shape, grad.dtype),
            pltpu.SemaphoreType.DMA((low.shape[0] // BLOCK,)),
            pltpu.VMEM((sum(p.shape[0] for p in parts), low.shape[1]), low.dtype),
        ],
        cost_estimate=COST,
        compiler_params=PARAMS,
        name="second_tile",
    )(scalars, place, low, grad, loss, raw, inv, *parts)


def first_tile(scalars, place, low, other, grad, loss, raw, inv, second_loss, outs):
    return pl.pallas_call(
        first_kernel,
        out_shape=(*like(grad, grad), jax.ShapeDtypeStruct(low.shape[:1], jnp.float32)),
        in_specs=[SMEM, SMEM] + [VMEM] * 7 + [ANY, ANY],
        out_specs=(ANY, ANY, VMEM),
        scratch_shapes=[pltpu.VMEM(grad.shape, grad.dtype), pltpu.SemaphoreType.DMA((low.shape[0] // BLOCK,))],
        input_output_aliases={9: 0, 10: 1},
        cost_estimate=COST,
        compiler_params=PARAMS,
        name="first_tile",
    )(scalars, place, low, other, grad, loss, raw, inv, second_loss, *outs)


def shards(image_embed, text_embed, logit_scale, logit_bias):
    scalars = jnp.concatenate([logit_scale, logit_bias])
    count = lax.axis_size("blk")
    facing = [(b, (b + 1) % count if b % 2 else (b - 1) % count) for b in range(count)]
    inside = [(b, b + 1 - 2 * (b % 2)) for b in range(count)]
    far = [(b, (b - 2) % count if b % 2 else (b + 2) % count) for b in range(count)]
    hold = lax.optimization_barrier
    parity = (lax.axis_index("blk") % 2).astype(jnp.int32)
    odd = parity == 1

    def across(value, part=PART):
        return [lax.ppermute(value[start : start + part], "blk", inside) for start in range(0, value.shape[0], part)]

    split = HEADS[0]
    first_a = hold(jnp.where(odd, text_embed[:split], image_embed[:split]))
    one_a = lax.ppermute(first_a, "blk", facing)
    image_embed, text_embed, first_a = hold((image_embed, text_embed, first_a))
    first_b = hold(jnp.where(odd, text_embed[split:], image_embed[split:]))
    one_b = lax.ppermute(first_b, "blk", facing)
    image_embed, text_embed, first_b = hold((image_embed, text_embed, first_b))
    second = hold(jnp.where(odd, image_embed, text_embed))
    zero = across(second)
    first, first_low, second_low, first_inv, second_inv, first_grad, second_grad, first_loss, second_loss = own_tile(
        scalars, first_a, first_b, second
    )
    second_grad, second_loss = add_tile(scalars, second_low, second_grad, second_loss, zero, True)

    one_a, second_loss = hold((one_a, second_loss))
    two_a = across(one_a)
    first_grad, first_loss = add_tile(scalars, first_low, first_grad, first_loss, [one_a], True)
    *two_a, first_loss = hold((*two_a, first_loss))
    second_grad, second_loss = add_tile(scalars, second_low, second_grad, second_loss, two_a, True)
    piece, second_loss = hold((second_low[: CUTS[0]], second_loss))
    late_a = lax.ppermute(piece, "blk", far)

    one_b, second_loss = hold((one_b, second_loss))
    two_b = across(one_b, TAIL_PART)
    piece, one_b = hold((second_low[-CUTS[1] :], one_b))
    late_b = lax.ppermute(piece, "blk", far)
    first_grad, first_loss = add_tile(scalars, first_low, first_grad, first_loss, [one_b], True)
    *two_b, first_loss = hold((*two_b, first_loss))
    *outs, second_loss = second_tile(scalars, 1 - parity[None], second_low, second_grad, second_loss, second, second_inv, two_b)
    late_a, second_loss = hold((late_a, second_loss))
    first_grad, first_loss = add_tile(scalars, first_low, first_grad, first_loss, [late_a], False)

    grad_image, grad_text, row_loss = first_tile(
        scalars, parity[None], first_low, late_b, first_grad, first_loss, first, first_inv, second_loss, outs
    )
    return (row_loss, grad_image, grad_text)


def solution(mesh):
    in_specs = (P(("dp", "blk"), None), P(("dp", "blk"), None), P(), P())
    out_specs = (P(("dp", "blk")), P(("dp", "blk"), None), P(("dp", "blk"), None))
    return jax.shard_map(shards, mesh=mesh, in_specs=in_specs, out_specs=out_specs, check_vma=False)
```

```python
import functools

import jax
import jax.numpy as jnp
from jax import lax
from jax.experimental import pallas as pl
from jax.experimental.pallas import tpu as pltpu
from jax.sharding import PartitionSpec as P

EPS = 1e-06
HEADS = (384, 384)
CUTS = (512, 256)
BLOCK = 384
LANES = 128
PART = 256
TAIL_PART = 192


def inverse_norm(x):
    return lax.rsqrt(jnp.sum(x * x, axis=-1, keepdims=True) + EPS)


def dot_rows(a, b):
    return lax.dot_general(a, b, (((1,), (1,)), ((), ())), preferred_element_type=jnp.float32)


def blocks(ref):
    step = ref.shape[0] // pl.cdiv(ref.shape[0], BLOCK)
    return [pl.ds(start, step) for start in range(0, ref.shape[0], step)]


def normalize_parts(parts, low):
    start = 0
    for part in parts:
        normalize_into(part, low.at[pl.ds(start, part.shape[0])])
        start += part.shape[0]


def normalize_into(raw, low, inv=None):
    for at in blocks(raw):
        x = raw[at, :].astype(jnp.float32)
        scaled = inverse_norm(x)
        low[at, :] = (x * scaled).astype(jnp.bfloat16)
        if inv is not None:
            inv[at, :] = scaled


def pair_terms(logits, scale, diagonal=None):
    if diagonal is not None:
        logits = jnp.where(diagonal, -logits, logits)
        scale = jnp.where(diagonal, -scale, scale)
    up = jnp.exp(logits)
    coef = (scale * (up / (1.0 + up))).astype(jnp.bfloat16)
    return coef, jnp.sum(jnp.log1p(up), axis=1, keepdims=True)


def own_kernel(scalars, first_a, first_b, second, first, first_low, second_low, first_inv, second_inv, first_grad, second_grad, first_loss, second_loss):
    scale, bias = scalars[0], scalars[1]
    split = first_a.shape[0]
    first[:split, :] = first_a[...]
    first[split:, :] = first_b[...]
    normalize_into(first, first_low, first_inv)
    normalize_into(second, second_low, second_inv)
    for low, other, grad, loss in (
        (first_low, second_low, first_grad, first_loss),
        (second_low, first_low, second_grad, second_loss),
    ):
        for at in blocks(low):
            logits = scale * dot_rows(low[at, :], other[...]) + bias
            row = at.start + lax.broadcasted_iota(jnp.int32, logits.shape, 0)
            diagonal = row == lax.broadcasted_iota(jnp.int32, logits.shape, 1)
            coef, loss[at, :] = pair_terms(logits, scale, diagonal)
            grad[at, :] = jnp.dot(coef, other[...], preferred_element_type=jnp.float32)


def coefficients(scalars, low, other):
    scale, bias = scalars[0], scalars[1]
    return [(at, *pair_terms(scale * dot_rows(low[at, :], other[...]) + bias, scale)) for at in blocks(low)]


def add_kernel(scalars, low, grad, loss, *rest):
    *parts, grad_out, loss_out, other = rest
    normalize_parts(parts, other)
    add_low_kernel(scalars, low, grad, loss, other, grad_out, loss_out)


def add_low_kernel(scalars, low, grad, loss, other, grad_out, loss_out):
    for at, coef, losses in coefficients(scalars, low, other):
        grad_out[at, :] = grad[at, :] + jnp.dot(coef, other[...], preferred_element_type=jnp.float32)
        loss_out[at, :] = loss[at, :] + losses


def finish(place, terms, other, grad, raw, inv, even_out, odd_out, held, sems):
    copies = []
    for step, (at, coef, _) in enumerate(terms):
        total = grad[at, :] + jnp.dot(coef, other[...], preferred_element_type=jnp.float32)
        unit = raw[at, :].astype(jnp.float32) * inv[at, :]
        held[at, :] = inv[at, :] * (total - unit * jnp.sum(unit * total, axis=-1, keepdims=True))
        copies.append([pltpu.make_async_copy(held.at[at], out.at[at], sems.at[step]) for out in (even_out, odd_out)])
        pl.when(place[0] == 0)(copies[-1][0].start)
        pl.when(place[0] != 0)(copies[-1][1].start)
    return copies


def wait_for(place, copies):
    for pair in copies:
        pl.when(place[0] == 0)(pair[0].wait)
        pl.when(place[0] != 0)(pair[1].wait)


def second_kernel(scalars, place, low, grad, loss, raw, inv, *rest):
    *parts, even_out, odd_out, loss_out, held, sems, other = rest
    normalize_parts(parts, other)
    terms = coefficients(scalars, low, other)
    copies = finish(place, terms, other, grad, raw, inv, even_out, odd_out, held, sems)
    for at, _, losses in terms:
        loss_out[at, :] = loss[at, :] + losses
    wait_for(place, copies)


def first_kernel(scalars, place, low, other, grad, loss, raw, inv, second_loss, even_in, odd_in, even_out, odd_out, loss_out, held, sems):
    terms = coefficients(scalars, low, other)
    copies = finish(place, terms, other, grad, raw, inv, even_out, odd_out, held, sems)
    for at, _, losses in terms:
        chosen = jnp.where(place[0] == 0, loss[at, :] + losses, second_loss[at, :]) / (3 * low.shape[0])
        loss_out[at] = jnp.transpose(jnp.broadcast_to(chosen, (BLOCK, LANES)))[0]
    wait_for(place, copies)


VMEM = pl.BlockSpec(memory_space=pltpu.VMEM)
SMEM = pl.BlockSpec(memory_space=pltpu.SMEM)
ANY = pl.BlockSpec(memory_space=pl.ANY)
PARAMS = pltpu.CompilerParams(vmem_limit_bytes=24 * 1024 * 1024)


COST = pl.CostEstimate(flops=1, bytes_accessed=1, transcendentals=0)


def like(*arrays):
    return tuple(jax.ShapeDtypeStruct(a.shape, a.dtype) for a in arrays)


def own_tile(scalars, first_a, first_b, second):
    grad = jax.ShapeDtypeStruct(second.shape, jnp.float32)
    column = jax.ShapeDtypeStruct((second.shape[0], 1), jnp.float32)
    return pl.pallas_call(
        own_kernel,
        out_shape=(*like(second, second, second), column, column, grad, grad, column, column),
        in_specs=[SMEM, VMEM, VMEM, VMEM],
        out_specs=(VMEM,) * 9,
        cost_estimate=COST,
        compiler_params=PARAMS,
        name="own_tile",
    )(scalars, first_a, first_b, second)


def add_tile(scalars, low, grad, loss, parts, raw):
    return pl.pallas_call(
        add_kernel if raw else add_low_kernel,
        out_shape=like(grad, loss),
        in_specs=[SMEM] + [VMEM] * (3 + len(parts)),
        out_specs=(VMEM, VMEM),
        scratch_shapes=[pltpu.VMEM((sum(p.shape[0] for p in parts), low.shape[1]), low.dtype)] if raw else [],
        input_output_aliases={2: 0, 3: 1},
        cost_estimate=COST,
        compiler_params=PARAMS,
        name="add_tile",
    )(scalars, low, grad, loss, *parts)


def second_tile(scalars, place, low, grad, loss, raw, inv, parts):
    return pl.pallas_call(
        second_kernel,
        out_shape=like(grad, grad, loss),
        in_specs=[SMEM, SMEM] + [VMEM] * (5 + len(parts)),
        out_specs=(ANY, ANY, VMEM),
        scratch_shapes=[
            pltpu.VMEM(grad.shape, grad.dtype),
            pltpu.SemaphoreType.DMA((low.shape[0] // BLOCK,)),
            pltpu.VMEM((sum(p.shape[0] for p in parts), low.shape[1]), low.dtype),
        ],
        cost_estimate=COST,
        compiler_params=PARAMS,
        name="second_tile",
    )(scalars, place, low, grad, loss, raw, inv, *parts)


def first_tile(scalars, place, low, other, grad, loss, raw, inv, second_loss, outs):
    return pl.pallas_call(
        first_kernel,
        out_shape=(*like(grad, grad), jax.ShapeDtypeStruct(low.shape[:1], jnp.float32)),
        in_specs=[SMEM, SMEM] + [VMEM] * 7 + [ANY, ANY],
        out_specs=(ANY, ANY, VMEM),
        scratch_shapes=[pltpu.VMEM(grad.shape, grad.dtype), pltpu.SemaphoreType.DMA((low.shape[0] // BLOCK,))],
        input_output_aliases={9: 0, 10: 1},
        cost_estimate=COST,
        compiler_params=PARAMS,
        name="first_tile",
    )(scalars, place, low, other, grad, loss, raw, inv, second_loss, *outs)


def shards(image_embed, text_embed, logit_scale, logit_bias):
    scalars = jnp.concatenate([logit_scale, logit_bias])
    count = lax.axis_size("blk")
    facing = [(b, (b + 1) % count if b % 2 else (b - 1) % count) for b in range(count)]
    inside = [(b, b + 1 - 2 * (b % 2)) for b in range(count)]
    far = [(b, (b - 2) % count if b % 2 else (b + 2) % count) for b in range(count)]
    hold = lax.optimization_barrier
    parity = (lax.axis_index("blk") % 2).astype(jnp.int32)
    odd = parity == 1

    def across(value, part=PART):
        return [lax.ppermute(value[start : start + part], "blk", inside) for start in range(0, value.shape[0], part)]

    split = HEADS[0]
    first_a = hold(jnp.where(odd, text_embed[:split], image_embed[:split]))
    one_a = lax.ppermute(first_a, "blk", facing)
    image_embed, text_embed, first_a = hold((image_embed, text_embed, first_a))
    first_b = hold(jnp.where(odd, text_embed[split:], image_embed[split:]))
    one_b = lax.ppermute(first_b, "blk", facing)
    image_embed, text_embed, first_b = hold((image_embed, text_embed, first_b))
    second = hold(jnp.where(odd, image_embed, text_embed))
    zero = across(second)
    first, first_low, second_low, first_inv, second_inv, first_grad, second_grad, first_loss, second_loss = own_tile(
        scalars, first_a, first_b, second
    )
    second_grad, second_loss = add_tile(scalars, second_low, second_grad, second_loss, zero, True)

    one_a, second_loss = hold((one_a, second_loss))
    two_a = across(one_a)
    first_grad, first_loss = add_tile(scalars, first_low, first_grad, first_loss, [one_a], True)
    piece, first_loss = hold((second_low[: CUTS[0]], first_loss))
    late_a = lax.ppermute(piece, "blk", far)
    *two_a, first_loss = hold((*two_a, first_loss))
    second_grad, second_loss = add_tile(scalars, second_low, second_grad, second_loss, two_a, True)

    one_b, second_loss = hold((one_b, second_loss))
    two_b = across(one_b, TAIL_PART)
    piece, one_b = hold((second_low[-CUTS[1] :], one_b))
    late_b = lax.ppermute(piece, "blk", far)
    first_grad, first_loss = add_tile(scalars, first_low, first_grad, first_loss, [one_b], True)
    *two_b, first_loss = hold((*two_b, first_loss))
    *outs, second_loss = second_tile(scalars, 1 - parity[None], second_low, second_grad, second_loss, second, second_inv, two_b)
    late_a, second_loss = hold((late_a, second_loss))
    first_grad, first_loss = add_tile(scalars, first_low, first_grad, first_loss, [late_a], False)

    grad_image, grad_text, row_loss = first_tile(
        scalars, parity[None], first_low, late_b, first_grad, first_loss, first, first_inv, second_loss, outs
    )
    return (row_loss, grad_image, grad_text)


def solution(mesh):
    in_specs = (P(("dp", "blk"), None), P(("dp", "blk"), None), P(), P())
    out_specs = (P(("dp", "blk")), P(("dp", "blk"), None), P(("dp", "blk"), None))
    return jax.shard_map(shards, mesh=mesh, in_specs=in_specs, out_specs=out_specs, check_vma=False)
```

```python
import functools

import jax
import jax.numpy as jnp
from jax import lax
from jax.experimental import pallas as pl
from jax.experimental.pallas import tpu as pltpu
from jax.sharding import PartitionSpec as P

EPS = 1e-06
HEADS = (384, 384)
CUTS = (512, 256)
BLOCK = 384
LANES = 128
PICKS = 4
PART = 256
TAIL_PART = 192


def inverse_norm(x):
    return lax.rsqrt(jnp.sum(x * x, axis=-1, keepdims=True) + EPS)


def dot_rows(a, b):
    return lax.dot_general(a, b, (((1,), (1,)), ((), ())), preferred_element_type=jnp.float32)


def blocks(ref):
    step = ref.shape[0] // pl.cdiv(ref.shape[0], BLOCK)
    return [pl.ds(start, step) for start in range(0, ref.shape[0], step)]


def normalize_parts(parts, low):
    start = 0
    for part in parts:
        normalize_into(part, low.at[pl.ds(start, part.shape[0])])
        start += part.shape[0]


def normalize_into(raw, low, inv=None):
    for at in blocks(raw):
        x = raw[at, :].astype(jnp.float32)
        scaled = inverse_norm(x)
        low[at, :] = (x * scaled).astype(jnp.bfloat16)
        if inv is not None:
            inv[at, :] = scaled


def pair_terms(logits, scale, diagonal=None):
    if diagonal is not None:
        logits = jnp.where(diagonal, -logits, logits)
        scale = jnp.where(diagonal, -scale, scale)
    up = jnp.exp(logits)
    coef = (scale * (up / (1.0 + up))).astype(jnp.bfloat16)
    return coef, jnp.sum(jnp.log1p(up), axis=1, keepdims=True)


def own_kernel(scalars, first_a, first_b, second, first, first_low, second_low, first_inv, second_inv, first_grad, second_grad, first_loss, second_loss):
    scale, bias = scalars[0], scalars[1]
    split = first_a.shape[0]
    first[:split, :] = first_a[...]
    first[split:, :] = first_b[...]
    normalize_into(first, first_low, first_inv)
    normalize_into(second, second_low, second_inv)
    for low, other, grad, loss in (
        (first_low, second_low, first_grad, first_loss),
        (second_low, first_low, second_grad, second_loss),
    ):
        for at in blocks(low):
            logits = scale * dot_rows(low[at, :], other[...]) + bias
            row = at.start + lax.broadcasted_iota(jnp.int32, logits.shape, 0)
            diagonal = row == lax.broadcasted_iota(jnp.int32, logits.shape, 1)
            coef, loss[at, :] = pair_terms(logits, scale, diagonal)
            grad[at, :] = jnp.dot(coef, other[...], preferred_element_type=jnp.float32)


def coefficients(scalars, low, other):
    scale, bias = scalars[0], scalars[1]
    return [(at, *pair_terms(scale * dot_rows(low[at, :], other[...]) + bias, scale)) for at in blocks(low)]


def add_kernel(scalars, low, grad, loss, *rest):
    *parts, grad_out, loss_out, other = rest
    normalize_parts(parts, other)
    add_low_kernel(scalars, low, grad, loss, other, grad_out, loss_out)


def add_low_kernel(scalars, low, grad, loss, other, grad_out, loss_out):
    for at, coef, losses in coefficients(scalars, low, other):
        grad_out[at, :] = grad[at, :] + jnp.dot(coef, other[...], preferred_element_type=jnp.float32)
        loss_out[at, :] = loss[at, :] + losses


def finish(place, terms, other, grad, raw, inv, even_out, odd_out, held, sems):
    copies = []
    for step, (at, coef, _) in enumerate(terms):
        total = grad[at, :] + jnp.dot(coef, other[...], preferred_element_type=jnp.float32)
        unit = raw[at, :].astype(jnp.float32) * inv[at, :]
        held[at, :] = inv[at, :] * (total - unit * jnp.sum(unit * total, axis=-1, keepdims=True))
        copies.append([pltpu.make_async_copy(held.at[at], out.at[at], sems.at[step]) for out in (even_out, odd_out)])
        pl.when(place[0] == 0)(copies[-1][0].start)
        pl.when(place[0] != 0)(copies[-1][1].start)
    return copies


def wait_for(place, copies):
    for pair in copies:
        pl.when(place[0] == 0)(pair[0].wait)
        pl.when(place[0] != 0)(pair[1].wait)


def second_kernel(scalars, place, low, grad, loss, raw, inv, *rest):
    *parts, even_out, odd_out, loss_out, held, sems, other = rest
    normalize_parts(parts, other)
    terms = coefficients(scalars, low, other)
    copies = finish(place, terms, other, grad, raw, inv, even_out, odd_out, held, sems)
    for at, _, losses in terms:
        loss_out[at, :] = loss[at, :] + losses
    wait_for(place, copies)


def first_kernel(scalars, place, low, other, grad, loss, raw, inv, second_loss, even_in, odd_in, even_out, odd_out, loss_out, held, sems, row, row_sem):
    terms = coefficients(scalars, low, other)
    for at, _, losses in terms:
        chosen = jnp.where(place[0] == 0, loss[at, :] + losses, second_loss[at, :]) / (3 * low.shape[0])
        row[at] = jnp.transpose(jnp.broadcast_to(chosen, (BLOCK, LANES)))[0]
    row_copy = pltpu.make_async_copy(row, loss_out, row_sem)
    row_copy.start()
    copies = finish(place, terms, other, grad, raw, inv, even_out, odd_out, held, sems)
    row_copy.wait()
    wait_for(place, copies)


VMEM = pl.BlockSpec(memory_space=pltpu.VMEM)
SMEM = pl.BlockSpec(memory_space=pltpu.SMEM)
ANY = pl.BlockSpec(memory_space=pl.ANY)
PARAMS = pltpu.CompilerParams(vmem_limit_bytes=24 * 1024 * 1024)


COST = pl.CostEstimate(flops=1, bytes_accessed=1, transcendentals=0)


def pick_kernel(image, text, out, sems):
    odd = lax.axis_index("blk") % 2 == 1
    rows = out.shape[0] // PICKS
    for source, wanted in ((image, jnp.logical_not(odd)), (text, odd)):
        pieces = [pl.ds(step * rows, rows) for step in range(PICKS)]
        copies = [pltpu.make_async_copy(source.at[at], out.at[at], sems.at[step]) for step, at in enumerate(pieces)]

        @pl.when(wanted)
        def _():
            for copy in copies:
                copy.start()
            for copy in copies:
                copy.wait()


def pick_rows(image, text, rows):
    return pl.pallas_call(
        pick_kernel,
        out_shape=jax.ShapeDtypeStruct((rows, image.shape[1]), image.dtype),
        in_specs=[ANY, ANY],
        out_specs=VMEM,
        scratch_shapes=[pltpu.SemaphoreType.DMA((PICKS,))],
        cost_estimate=COST,
        compiler_params=PARAMS,
        name="pick_rows",
    )(image, text)


def like(*arrays):
    return tuple(jax.ShapeDtypeStruct(a.shape, a.dtype) for a in arrays)


def own_tile(scalars, first_a, first_b, second):
    grad = jax.ShapeDtypeStruct(second.shape, jnp.float32)
    column = jax.ShapeDtypeStruct((second.shape[0], 1), jnp.float32)
    return pl.pallas_call(
        own_kernel,
        out_shape=(*like(second, second, second), column, column, grad, grad, column, column),
        in_specs=[SMEM, VMEM, VMEM, VMEM],
        out_specs=(VMEM,) * 9,
        cost_estimate=COST,
        compiler_params=PARAMS,
        name="own_tile",
    )(scalars, first_a, first_b, second)


def add_tile(scalars, low, grad, loss, parts, raw):
    return pl.pallas_call(
        add_kernel if raw else add_low_kernel,
        out_shape=like(grad, loss),
        in_specs=[SMEM] + [VMEM] * (3 + len(parts)),
        out_specs=(VMEM, VMEM),
        scratch_shapes=[pltpu.VMEM((sum(p.shape[0] for p in parts), low.shape[1]), low.dtype)] if raw else [],
        input_output_aliases={2: 0, 3: 1},
        cost_estimate=COST,
        compiler_params=PARAMS,
        name="add_tile",
    )(scalars, low, grad, loss, *parts)


def second_tile(scalars, place, low, grad, loss, raw, inv, parts):
    return pl.pallas_call(
        second_kernel,
        out_shape=like(grad, grad, loss),
        in_specs=[SMEM, SMEM] + [VMEM] * (5 + len(parts)),
        out_specs=(ANY, ANY, VMEM),
        scratch_shapes=[
            pltpu.VMEM(grad.shape, grad.dtype),
            pltpu.SemaphoreType.DMA((low.shape[0] // BLOCK,)),
            pltpu.VMEM((sum(p.shape[0] for p in parts), low.shape[1]), low.dtype),
        ],
        cost_estimate=COST,
        compiler_params=PARAMS,
        name="second_tile",
    )(scalars, place, low, grad, loss, raw, inv, *parts)


def first_tile(scalars, place, low, other, grad, loss, raw, inv, second_loss, outs):
    return pl.pallas_call(
        first_kernel,
        out_shape=(*like(grad, grad), jax.ShapeDtypeStruct(low.shape[:1], jnp.float32)),
        in_specs=[SMEM, SMEM] + [VMEM] * 7 + [ANY, ANY],
        out_specs=(ANY, ANY, ANY),
        scratch_shapes=[
            pltpu.VMEM(grad.shape, grad.dtype),
            pltpu.SemaphoreType.DMA((low.shape[0] // BLOCK,)),
            pltpu.VMEM(low.shape[:1], jnp.float32),
            pltpu.SemaphoreType.DMA(()),
        ],
        input_output_aliases={9: 0, 10: 1},
        cost_estimate=COST,
        compiler_params=PARAMS,
        name="first_tile",
    )(scalars, place, low, other, grad, loss, raw, inv, second_loss, *outs)


def shards(image_embed, text_embed, logit_scale, logit_bias):
    scalars = jnp.concatenate([logit_scale, logit_bias])
    count = lax.axis_size("blk")
    facing = [(b, (b + 1) % count if b % 2 else (b - 1) % count) for b in range(count)]
    inside = [(b, b + 1 - 2 * (b % 2)) for b in range(count)]
    far = [(b, (b - 2) % count if b % 2 else (b + 2) % count) for b in range(count)]
    hold = lax.optimization_barrier
    parity = (lax.axis_index("blk") % 2).astype(jnp.int32)
    odd = parity == 1

    def across(value, part=PART):
        return [lax.ppermute(value[start : start + part], "blk", inside) for start in range(0, value.shape[0], part)]

    split = HEADS[0]
    first_a = pick_rows(image_embed, text_embed, split)
    one_a = lax.ppermute(first_a, "blk", facing)
    image_embed, text_embed, first_a = hold((image_embed, text_embed, first_a))
    first_b = hold(jnp.where(odd, text_embed[split:], image_embed[split:]))
    one_b = lax.ppermute(first_b, "blk", facing)
    image_embed, text_embed, first_b = hold((image_embed, text_embed, first_b))
    second = hold(jnp.where(odd, image_embed, text_embed))
    zero = across(second)
    first, first_low, second_low, first_inv, second_inv, first_grad, second_grad, first_loss, second_loss = own_tile(
        scalars, first_a, first_b, second
    )
    second_grad, second_loss = add_tile(scalars, second_low, second_grad, second_loss, zero, True)

    one_a, second_loss = hold((one_a, second_loss))
    two_a = across(one_a)
    first_grad, first_loss = add_tile(scalars, first_low, first_grad, first_loss, [one_a], True)
    piece, first_loss = hold((second_low[: CUTS[0]], first_loss))
    late_a = lax.ppermute(piece, "blk", far)
    *two_a, first_loss = hold((*two_a, first_loss))
    second_grad, second_loss = add_tile(scalars, second_low, second_grad, second_loss, two_a, True)

    one_b, second_loss = hold((one_b, second_loss))
    two_b = across(one_b, TAIL_PART)
    piece, one_b = hold((second_low[-CUTS[1] :], one_b))
    late_b = lax.ppermute(piece, "blk", far)
    first_grad, first_loss = add_tile(scalars, first_low, first_grad, first_loss, [one_b], True)
    *two_b, first_loss = hold((*two_b, first_loss))
    *outs, second_loss = second_tile(scalars, 1 - parity[None], second_low, second_grad, second_loss, second, second_inv, two_b)
    late_a, second_loss = hold((late_a, second_loss))
    first_grad, first_loss = add_tile(scalars, first_low, first_grad, first_loss, [late_a], False)

    grad_image, grad_text, row_loss = first_tile(
        scalars, parity[None], first_low, late_b, first_grad, first_loss, first, first_inv, second_loss, outs
    )
    return (row_loss, grad_image, grad_text)


def solution(mesh):
    in_specs = (P(("dp", "blk"), None), P(("dp", "blk"), None), P(), P())
    out_specs = (P(("dp", "blk")), P(("dp", "blk"), None), P(("dp", "blk"), None))
    return jax.shard_map(shards, mesh=mesh, in_specs=in_specs, out_specs=out_specs, check_vma=False)
```

```python
import functools

import jax
import jax.numpy as jnp
from jax import lax
from jax.experimental import pallas as pl
from jax.experimental.pallas import tpu as pltpu
from jax.sharding import PartitionSpec as P

EPS = 1e-06
HEADS = (384, 384)
CUTS = (512, 256)
BLOCK = 384
LANES = 128
PART = 256
TAIL_PART = 192


def inverse_norm(x):
    return lax.rsqrt(jnp.sum(x * x, axis=-1, keepdims=True) + EPS)


def dot_rows(a, b):
    return lax.dot_general(a, b, (((1,), (1,)), ((), ())), preferred_element_type=jnp.float32)


def blocks(ref):
    step = ref.shape[0] // pl.cdiv(ref.shape[0], BLOCK)
    return [pl.ds(start, step) for start in range(0, ref.shape[0], step)]


def normalize_parts(parts, low):
    start = 0
    for part in parts:
        normalize_into(part, low.at[pl.ds(start, part.shape[0])])
        start += part.shape[0]


def normalize_into(raw, low, inv=None):
    for at in blocks(raw):
        x = raw[at, :].astype(jnp.float32)
        scaled = inverse_norm(x)
        low[at, :] = (x * scaled).astype(jnp.bfloat16)
        if inv is not None:
            inv[at, :] = scaled


def pair_terms(logits, scale, diagonal=None):
    if diagonal is not None:
        logits = jnp.where(diagonal, -logits, logits)
        scale = jnp.where(diagonal, -scale, scale)
    up = jnp.exp(logits)
    coef = (scale * (up / (1.0 + up))).astype(jnp.bfloat16)
    return coef, jnp.sum(jnp.log1p(up), axis=1, keepdims=True)


def own_kernel(scalars, first_a, first_b, second, first, first_low, second_low, first_inv, second_inv, first_grad, second_grad, first_loss, second_loss):
    scale, bias = scalars[0], scalars[1]
    split = first_a.shape[0]
    first[:split, :] = first_a[...]
    first[split:, :] = first_b[...]
    normalize_into(first, first_low, first_inv)
    normalize_into(second, second_low, second_inv)
    for low, other, grad, loss in (
        (first_low, second_low, first_grad, first_loss),
        (second_low, first_low, second_grad, second_loss),
    ):
        for at in blocks(low):
            logits = scale * dot_rows(low[at, :], other[...]) + bias
            row = at.start + lax.broadcasted_iota(jnp.int32, logits.shape, 0)
            diagonal = row == lax.broadcasted_iota(jnp.int32, logits.shape, 1)
            coef, loss[at, :] = pair_terms(logits, scale, diagonal)
            grad[at, :] = jnp.dot(coef, other[...], preferred_element_type=jnp.float32)


def coefficients(scalars, low, other):
    scale, bias = scalars[0], scalars[1]
    return [(at, *pair_terms(scale * dot_rows(low[at, :], other[...]) + bias, scale)) for at in blocks(low)]


def add_kernel(scalars, low, grad, loss, *rest):
    *parts, grad_out, loss_out, other = rest
    normalize_parts(parts, other)
    add_low_kernel(scalars, low, grad, loss, other, grad_out, loss_out)


def add_low_kernel(scalars, low, grad, loss, other, grad_out, loss_out):
    for at, coef, losses in coefficients(scalars, low, other):
        grad_out[at, :] = grad[at, :] + jnp.dot(coef, other[...], preferred_element_type=jnp.float32)
        loss_out[at, :] = loss[at, :] + losses


def finish(even, terms, other, grad, raw, inv, even_out, odd_out, held, sems):
    copies = []
    for step, (at, coef, _) in enumerate(terms):
        total = grad[at, :] + jnp.dot(coef, other[...], preferred_element_type=jnp.float32)
        unit = raw[at, :].astype(jnp.float32) * inv[at, :]
        held[at, :] = inv[at, :] * (total - unit * jnp.sum(unit * total, axis=-1, keepdims=True))
        copies.append([pltpu.make_async_copy(held.at[at], out.at[at], sems.at[step]) for out in (even_out, odd_out)])
        pl.when(even)(copies[-1][0].start)
        pl.when(jnp.logical_not(even))(copies[-1][1].start)
    return copies


def wait_for(even, copies):
    for pair in copies:
        pl.when(even)(pair[0].wait)
        pl.when(jnp.logical_not(even))(pair[1].wait)


def second_kernel(scalars, low, grad, loss, raw, inv, *rest):
    *parts, even_out, odd_out, loss_out, held, sems, other = rest
    normalize_parts(parts, other)
    even = scalars[2] != 0
    terms = coefficients(scalars, low, other)
    copies = finish(even, terms, other, grad, raw, inv, even_out, odd_out, held, sems)
    for at, _, losses in terms:
        loss_out[at, :] = loss[at, :] + losses
    wait_for(even, copies)


def first_kernel(scalars, low, other, grad, loss, raw, inv, second_loss, even_in, odd_in, even_out, odd_out, loss_out, held, sems, row, row_sem):
    even = scalars[2] == 0
    terms = coefficients(scalars, low, other)
    for at, _, losses in terms:
        chosen = jnp.where(even, loss[at, :] + losses, second_loss[at, :]) / (3 * low.shape[0])
        row[at] = jnp.transpose(jnp.broadcast_to(chosen, (BLOCK, LANES)))[0]
    row_copy = pltpu.make_async_copy(row, loss_out, row_sem)
    row_copy.start()
    copies = finish(even, terms, other, grad, raw, inv, even_out, odd_out, held, sems)
    row_copy.wait()
    wait_for(even, copies)


VMEM = pl.BlockSpec(memory_space=pltpu.VMEM)
SMEM = pl.BlockSpec(memory_space=pltpu.SMEM)
ANY = pl.BlockSpec(memory_space=pl.ANY)
PARAMS = pltpu.CompilerParams(vmem_limit_bytes=24 * 1024 * 1024)


COST = pl.CostEstimate(flops=1, bytes_accessed=1, transcendentals=0)


def like(*arrays):
    return tuple(jax.ShapeDtypeStruct(a.shape, a.dtype) for a in arrays)


def own_tile(scalars, first_a, first_b, second):
    grad = jax.ShapeDtypeStruct(second.shape, jnp.float32)
    column = jax.ShapeDtypeStruct((second.shape[0], 1), jnp.float32)
    return pl.pallas_call(
        own_kernel,
        out_shape=(*like(second, second, second), column, column, grad, grad, column, column),
        in_specs=[SMEM, VMEM, VMEM, VMEM],
        out_specs=(VMEM,) * 9,
        cost_estimate=COST,
        compiler_params=PARAMS,
        name="own_tile",
    )(scalars, first_a, first_b, second)


def add_tile(scalars, low, grad, loss, parts, raw):
    return pl.pallas_call(
        add_kernel if raw else add_low_kernel,
        out_shape=like(grad, loss),
        in_specs=[SMEM] + [VMEM] * (3 + len(parts)),
        out_specs=(VMEM, VMEM),
        scratch_shapes=[pltpu.VMEM((sum(p.shape[0] for p in parts), low.shape[1]), low.dtype)] if raw else [],
        input_output_aliases={2: 0, 3: 1},
        cost_estimate=COST,
        compiler_params=PARAMS,
        name="add_tile",
    )(scalars, low, grad, loss, *parts)


def second_tile(scalars, low, grad, loss, raw, inv, parts):
    return pl.pallas_call(
        second_kernel,
        out_shape=like(grad, grad, loss),
        in_specs=[SMEM] + [VMEM] * (5 + len(parts)),
        out_specs=(ANY, ANY, VMEM),
        scratch_shapes=[
            pltpu.VMEM(grad.shape, grad.dtype),
            pltpu.SemaphoreType.DMA((low.shape[0] // BLOCK,)),
            pltpu.VMEM((sum(p.shape[0] for p in parts), low.shape[1]), low.dtype),
        ],
        cost_estimate=COST,
        compiler_params=PARAMS,
        name="second_tile",
    )(scalars, low, grad, loss, raw, inv, *parts)


def first_tile(scalars, low, other, grad, loss, raw, inv, second_loss, outs):
    return pl.pallas_call(
        first_kernel,
        out_shape=(*like(grad, grad), jax.ShapeDtypeStruct(low.shape[:1], jnp.float32)),
        in_specs=[SMEM] + [VMEM] * 7 + [ANY, ANY],
        out_specs=(ANY, ANY, ANY),
        scratch_shapes=[
            pltpu.VMEM(grad.shape, grad.dtype),
            pltpu.SemaphoreType.DMA((low.shape[0] // BLOCK,)),
            pltpu.VMEM(low.shape[:1], jnp.float32),
            pltpu.SemaphoreType.DMA(()),
        ],
        input_output_aliases={8: 0, 9: 1},
        cost_estimate=COST,
        compiler_params=PARAMS,
        name="first_tile",
    )(scalars, low, other, grad, loss, raw, inv, second_loss, *outs)


def shards(image_embed, text_embed, logit_scale, logit_bias):
    count = lax.axis_size("blk")
    facing = [(b, (b + 1) % count if b % 2 else (b - 1) % count) for b in range(count)]
    inside = [(b, b + 1 - 2 * (b % 2)) for b in range(count)]
    far = [(b, (b - 2) % count if b % 2 else (b + 2) % count) for b in range(count)]
    hold = lax.optimization_barrier
    parity = (lax.axis_index("blk") % 2).astype(jnp.int32)
    odd = parity == 1
    scalars = jnp.concatenate([logit_scale, logit_bias, parity[None].astype(jnp.float32)])

    def across(value, part=PART):
        return [lax.ppermute(value[start : start + part], "blk", inside) for start in range(0, value.shape[0], part)]

    split = HEADS[0]
    first_a = hold(jnp.where(odd, text_embed[:split], image_embed[:split]))
    one_a = lax.ppermute(first_a, "blk", facing)
    image_embed, text_embed, first_a = hold((image_embed, text_embed, first_a))
    first_b = hold(jnp.where(odd, text_embed[split:], image_embed[split:]))
    one_b = lax.ppermute(first_b, "blk", facing)
    image_embed, text_embed, first_b = hold((image_embed, text_embed, first_b))
    second = hold(jnp.where(odd, image_embed, text_embed))
    zero = across(second)
    first, first_low, second_low, first_inv, second_inv, first_grad, second_grad, first_loss, second_loss = own_tile(
        scalars, first_a, first_b, second
    )
    second_grad, second_loss = add_tile(scalars, second_low, second_grad, second_loss, zero, True)

    one_a, second_loss = hold((one_a, second_loss))
    two_a = across(one_a)
    first_grad, first_loss = add_tile(scalars, first_low, first_grad, first_loss, [one_a], True)
    piece, first_loss = hold((second_low[: CUTS[0]], first_loss))
    late_a = lax.ppermute(piece, "blk", far)
    *two_a, first_loss = hold((*two_a, first_loss))
    second_grad, second_loss = add_tile(scalars, second_low, second_grad, second_loss, two_a, True)

    one_b, second_loss = hold((one_b, second_loss))
    two_b = across(one_b, TAIL_PART)
    piece, one_b = hold((second_low[-CUTS[1] :], one_b))
    late_b = lax.ppermute(piece, "blk", far)
    first_grad, first_loss = add_tile(scalars, first_low, first_grad, first_loss, [one_b], True)
    *two_b, first_loss = hold((*two_b, first_loss))
    *outs, second_loss = second_tile(scalars, second_low, second_grad, second_loss, second, second_inv, two_b)
    late_a, second_loss = hold((late_a, second_loss))
    first_grad, first_loss = add_tile(scalars, first_low, first_grad, first_loss, [late_a], False)

    grad_image, grad_text, row_loss = first_tile(
        scalars, first_low, late_b, first_grad, first_loss, first, first_inv, second_loss, outs
    )
    return (row_loss, grad_image, grad_text)


def solution(mesh):
    in_specs = (P(("dp", "blk"), None), P(("dp", "blk"), None), P(), P())
    out_specs = (P(("dp", "blk")), P(("dp", "blk"), None), P(("dp", "blk"), None))
    return jax.shard_map(shards, mesh=mesh, in_specs=in_specs, out_specs=out_specs, check_vma=False)
```

```python
import functools

import jax
import jax.numpy as jnp
from jax import lax
from jax.experimental import pallas as pl
from jax.experimental.pallas import tpu as pltpu
from jax.sharding import PartitionSpec as P

EPS = 1e-06
HEADS = (384, 384)
CUTS = (512, 256)
BLOCK = 384
LANES = 128
PART = 256
TAIL_PART = 192


def inverse_norm(x):
    return lax.rsqrt(jnp.sum(x * x, axis=-1, keepdims=True) + EPS)


def dot_rows(a, b):
    return lax.dot_general(a, b, (((1,), (1,)), ((), ())), preferred_element_type=jnp.float32)


def blocks(ref):
    step = ref.shape[0] // pl.cdiv(ref.shape[0], BLOCK)
    return [pl.ds(start, step) for start in range(0, ref.shape[0], step)]


def normalize_parts(parts, low):
    start = 0
    for part in parts:
        normalize_into(part, low.at[pl.ds(start, part.shape[0])])
        start += part.shape[0]


def normalize_into(raw, low, inv=None):
    for at in blocks(raw):
        x = raw[at, :].astype(jnp.float32)
        scaled = inverse_norm(x)
        low[at, :] = (x * scaled).astype(jnp.bfloat16)
        if inv is not None:
            inv[at, :] = scaled


def pair_terms(logits, scale, diagonal=None):
    if diagonal is not None:
        logits = jnp.where(diagonal, -logits, logits)
        scale = jnp.where(diagonal, -scale, scale)
    up = jnp.exp(logits)
    coef = (scale * (up / (1.0 + up))).astype(jnp.bfloat16)
    return coef, jnp.sum(jnp.log1p(up), axis=1, keepdims=True)


def own_kernel(scalars, first_a, first_b, second, first, first_low, second_low, first_inv, second_inv, first_grad, second_grad, first_loss, second_loss):
    scale, bias = scalars[0], scalars[1]
    split = first_a.shape[0]
    first[:split, :] = first_a[...]
    first[split:, :] = first_b[...]
    normalize_into(first, first_low, first_inv)
    normalize_into(second, second_low, second_inv)
    for low, other, grad, loss in (
        (first_low, second_low, first_grad, first_loss),
        (second_low, first_low, second_grad, second_loss),
    ):
        for at in blocks(low):
            logits = scale * dot_rows(low[at, :], other[...]) + bias
            row = at.start + lax.broadcasted_iota(jnp.int32, logits.shape, 0)
            diagonal = row == lax.broadcasted_iota(jnp.int32, logits.shape, 1)
            coef, loss[at, :] = pair_terms(logits, scale, diagonal)
            grad[at, :] = jnp.dot(coef, other[...], preferred_element_type=jnp.float32)


def coefficients(scalars, low, other):
    scale, bias = scalars[0], scalars[1]
    return [(at, *pair_terms(scale * dot_rows(low[at, :], other[...]) + bias, scale)) for at in blocks(low)]


def add_kernel(scalars, low, grad, loss, *rest):
    *parts, grad_out, loss_out, other = rest
    normalize_parts(parts, other)
    add_low_kernel(scalars, low, grad, loss, other, grad_out, loss_out)


def add_low_kernel(scalars, low, grad, loss, other, grad_out, loss_out):
    for at, coef, losses in coefficients(scalars, low, other):
        grad_out[at, :] = grad[at, :] + jnp.dot(coef, other[...], preferred_element_type=jnp.float32)
        loss_out[at, :] = loss[at, :] + losses


def finish(even, terms, other, grad, raw, inv, even_out, odd_out, held, sems):
    copies = []
    for step, (at, coef, _) in enumerate(terms):
        total = grad[at, :] + jnp.dot(coef, other[...], preferred_element_type=jnp.float32)
        unit = raw[at, :].astype(jnp.float32) * inv[at, :]
        held[at, :] = inv[at, :] * (total - unit * jnp.sum(unit * total, axis=-1, keepdims=True))
        copies.append([pltpu.make_async_copy(held.at[at], out.at[at], sems.at[step]) for out in (even_out, odd_out)])
        pl.when(even)(copies[-1][0].start)
        pl.when(jnp.logical_not(even))(copies[-1][1].start)
    return copies


def wait_for(even, copies):
    for pair in copies:
        pl.when(even)(pair[0].wait)
        pl.when(jnp.logical_not(even))(pair[1].wait)


def second_kernel(scalars, low, grad, loss, raw, inv, *rest):
    *parts, even_out, odd_out, loss_out, held, sems, other = rest
    normalize_parts(parts, other)
    even = scalars[2] != 0
    terms = coefficients(scalars, low, other)
    copies = finish(even, terms, other, grad, raw, inv, even_out, odd_out, held, sems)
    for at, _, losses in terms:
        loss_out[at, :] = loss[at, :] + losses
    wait_for(even, copies)


def first_kernel(scalars, low, other, grad, loss, raw, inv, second_loss, even_in, odd_in, even_out, odd_out, loss_out, held, sems, row, row_sem):
    even = scalars[2] == 0
    terms = coefficients(scalars, low, other)
    for at, _, losses in terms:
        chosen = jnp.where(even, loss[at, :] + losses, second_loss[at, :]) / (3 * low.shape[0])
        row[at] = jnp.transpose(jnp.broadcast_to(chosen, (BLOCK, LANES)))[0]
    row_copy = pltpu.make_async_copy(row, loss_out, row_sem)
    row_copy.start()
    copies = finish(even, terms, other, grad, raw, inv, even_out, odd_out, held, sems)
    row_copy.wait()
    wait_for(even, copies)


VMEM = pl.BlockSpec(memory_space=pltpu.VMEM)
SMEM = pl.BlockSpec(memory_space=pltpu.SMEM)
ANY = pl.BlockSpec(memory_space=pl.ANY)
PARAMS = pltpu.CompilerParams(vmem_limit_bytes=20 * 1024 * 1024)


COST = pl.CostEstimate(flops=1, bytes_accessed=1, transcendentals=0)


def like(*arrays):
    return tuple(jax.ShapeDtypeStruct(a.shape, a.dtype) for a in arrays)


def own_tile(scalars, first_a, first_b, second):
    grad = jax.ShapeDtypeStruct(second.shape, jnp.float32)
    column = jax.ShapeDtypeStruct((second.shape[0], 1), jnp.float32)
    return pl.pallas_call(
        own_kernel,
        out_shape=(*like(second, second, second), column, column, grad, grad, column, column),
        in_specs=[SMEM, VMEM, VMEM, VMEM],
        out_specs=(VMEM,) * 9,
        cost_estimate=COST,
        compiler_params=PARAMS,
        name="own_tile",
    )(scalars, first_a, first_b, second)


def add_tile(scalars, low, grad, loss, parts, raw):
    return pl.pallas_call(
        add_kernel if raw else add_low_kernel,
        out_shape=like(grad, loss),
        in_specs=[SMEM] + [VMEM] * (3 + len(parts)),
        out_specs=(VMEM, VMEM),
        scratch_shapes=[pltpu.VMEM((sum(p.shape[0] for p in parts), low.shape[1]), low.dtype)] if raw else [],
        input_output_aliases={2: 0, 3: 1},
        cost_estimate=COST,
        compiler_params=PARAMS,
        name="add_tile",
    )(scalars, low, grad, loss, *parts)


def second_tile(scalars, low, grad, loss, raw, inv, parts):
    return pl.pallas_call(
        second_kernel,
        out_shape=like(grad, grad, loss),
        in_specs=[SMEM] + [VMEM] * (5 + len(parts)),
        out_specs=(ANY, ANY, VMEM),
        scratch_shapes=[
            pltpu.VMEM(grad.shape, grad.dtype),
            pltpu.SemaphoreType.DMA((low.shape[0] // BLOCK,)),
            pltpu.VMEM((sum(p.shape[0] for p in parts), low.shape[1]), low.dtype),
        ],
        cost_estimate=COST,
        compiler_params=PARAMS,
        name="second_tile",
    )(scalars, low, grad, loss, raw, inv, *parts)


def first_tile(scalars, low, other, grad, loss, raw, inv, second_loss, outs):
    return pl.pallas_call(
        first_kernel,
        out_shape=(*like(grad, grad), jax.ShapeDtypeStruct(low.shape[:1], jnp.float32)),
        in_specs=[SMEM] + [VMEM] * 7 + [ANY, ANY],
        out_specs=(ANY, ANY, ANY),
        scratch_shapes=[
            pltpu.VMEM(grad.shape, grad.dtype),
            pltpu.SemaphoreType.DMA((low.shape[0] // BLOCK,)),
            pltpu.VMEM(low.shape[:1], jnp.float32),
            pltpu.SemaphoreType.DMA(()),
        ],
        input_output_aliases={8: 0, 9: 1},
        cost_estimate=COST,
        compiler_params=PARAMS,
        name="first_tile",
    )(scalars, low, other, grad, loss, raw, inv, second_loss, *outs)


def shards(image_embed, text_embed, logit_scale, logit_bias):
    count = lax.axis_size("blk")
    facing = [(b, (b + 1) % count if b % 2 else (b - 1) % count) for b in range(count)]
    inside = [(b, b + 1 - 2 * (b % 2)) for b in range(count)]
    far = [(b, (b - 2) % count if b % 2 else (b + 2) % count) for b in range(count)]
    hold = lax.optimization_barrier
    parity = (lax.axis_index("blk") % 2).astype(jnp.int32)
    odd = parity == 1
    scalars = jnp.concatenate([logit_scale, logit_bias, parity[None].astype(jnp.float32)])

    def across(value, part=PART):
        return [lax.ppermute(value[start : start + part], "blk", inside) for start in range(0, value.shape[0], part)]

    split = HEADS[0]
    first_a = hold(jnp.where(odd, text_embed[:split], image_embed[:split]))
    one_a = lax.ppermute(first_a, "blk", facing)
    image_embed, text_embed, first_a = hold((image_embed, text_embed, first_a))
    first_b = hold(jnp.where(odd, text_embed[split:], image_embed[split:]))
    one_b = lax.ppermute(first_b, "blk", facing)
    image_embed, text_embed, first_b = hold((image_embed, text_embed, first_b))
    second = hold(jnp.where(odd, image_embed, text_embed))
    zero = across(second)
    first, first_low, second_low, first_inv, second_inv, first_grad, second_grad, first_loss, second_loss = own_tile(
        scalars, first_a, first_b, second
    )
    second_grad, second_loss = add_tile(scalars, second_low, second_grad, second_loss, zero, True)

    one_a, second_loss = hold((one_a, second_loss))
    two_a = across(one_a)
    first_grad, first_loss = add_tile(scalars, first_low, first_grad, first_loss, [one_a], True)
    piece, first_loss = hold((second_low[: CUTS[0]], first_loss))
    late_a = lax.ppermute(piece, "blk", far)
    *two_a, first_loss = hold((*two_a, first_loss))
    second_grad, second_loss = add_tile(scalars, second_low, second_grad, second_loss, two_a, True)

    one_b, second_loss = hold((one_b, second_loss))
    two_b = across(one_b, TAIL_PART)
    piece, one_b = hold((second_low[-CUTS[1] :], one_b))
    late_b = lax.ppermute(piece, "blk", far)
    first_grad, first_loss = add_tile(scalars, first_low, first_grad, first_loss, [one_b], True)
    *two_b, first_loss = hold((*two_b, first_loss))
    *outs, second_loss = second_tile(scalars, second_low, second_grad, second_loss, second, second_inv, two_b)
    late_a, second_loss = hold((late_a, second_loss))
    first_grad, first_loss = add_tile(scalars, first_low, first_grad, first_loss, [late_a], False)

    grad_image, grad_text, row_loss = first_tile(
        scalars, first_low, late_b, first_grad, first_loss, first, first_inv, second_loss, outs
    )
    return (row_loss, grad_image, grad_text)


def solution(mesh):
    in_specs = (P(("dp", "blk"), None), P(("dp", "blk"), None), P(), P())
    out_specs = (P(("dp", "blk")), P(("dp", "blk"), None), P(("dp", "blk"), None))
    return jax.shard_map(shards, mesh=mesh, in_specs=in_specs, out_specs=out_specs, check_vma=False)
```
